256 devices in a mesh: cplx: 8 (over y, core), grp: 32 (over z, x).
Axes of the slice: x: 4, y: 4, z: 8, core: 2. Of those that a mesh axis runs over, the one named last changes fastest.
Arguments:
- sequence_stack: bfloat16 [8, 512, 256, 256], P('cplx', 'grp'), may hold values from -6 to 6
- depths: int32 [8], replicated, may hold values from 64 to 512, as said below
- standardize_factor: float32 [256], replicated, may hold values from 0.1 to 1.9
- standardize_shift: float32 [256], replicated, may hold values from -1.5 to 1.5
- input_weight: bfloat16 [256, 1024], P(None, 'cplx')
- sigmoid_shift: float32 [256], replicated, may hold values from -4 to 4
- result_matrix: bfloat16 [256, 256], P('cplx'), may hold values from -0.375 to 0.375
- result_shift: float32 [256], replicated, may hold values from -1.5 to 1.5
Outputs:
- msa_out: bfloat16 [8, 512, 256, 256], P('cplx', 'grp')
The draws below stay inside these ranges and needn't reach their ends.
Inputs may be any that keep to these rules, and one draw needn't show every extreme that they name: `depths`: one complex has exactly 512 rows and one exactly 64.
All inputs are finite; a program needn't handle non-finite values.
Results may differ from the reference program's by a relative error of at most 0.0034.
The reference program's roundings to bfloat16 on the way count: a program that leaves them out, or rounds other values in their place, can miss the bound.
Values may be sent and summed in bfloat16 or wider, within the bound.
No kernel may reach another device: no remote copies, remote signals or barrier semaphores. Data moves between devices by JAX's collectives and lax.ppermute only.
A program may use at most 192 MiB of HBM per device.

```python
import math
import jax
import jax.numpy as jnp
from jax import lax

FEATURE_DEPTH = 256
FOCUS_PATHS = 8
WINDOW_LENGTH = 256
SEQUENCE_LIMIT = 512
ASSEMBLY_TOTAL = 8


def draw_depths(key, part):
    key = jax.random.fold_in(key, 11)
    depth_key, shuffle_key = jax.random.split(key)
    lowest = SEQUENCE_LIMIT // 8
    drawn_depths = jax.random.randint(depth_key, (ASSEMBLY_TOTAL,), lowest, SEQUENCE_LIMIT + 1)
    shuffled = jax.random.permutation(shuffle_key, ASSEMBLY_TOTAL)
    drawn_depths = drawn_depths.at[shuffled[0]].set(SEQUENCE_LIMIT)
    drawn_depths = drawn_depths.at[shuffled[1]].set(lowest)
    return drawn_depths.astype(jnp.int32)


def draw_input_weight(key, part):
    key = jax.random.fold_in(key, 23)
    random_seed, boost_key = jax.random.split(key)
    initial_sequences = jnp.clip(jax.random.normal(random_seed, (FEATURE_DEPTH, 4 * FEATURE_DEPTH), jnp.float32), -5.0, 5.0) / math.sqrt(FEATURE_DEPTH)
    path_dimension = FEATURE_DEPTH // FOCUS_PATHS
    logit_raises = jax.random.uniform(boost_key, (2, FOCUS_PATHS), jnp.float32, 1.2, 1.8)
    position_raise = jnp.concatenate([jnp.repeat(logit_raises, path_dimension, axis=1).reshape(2 * FEATURE_DEPTH), jnp.ones((2 * FEATURE_DEPTH,), jnp.float32)])
    return (initial_sequences * position_raise[None, :]).astype(jnp.bfloat16)


def block_scale(own_key, dims, cuts, least, high):
    gain = 1.0
    for position, blocks in cuts:
        heights = jax.random.uniform(jax.random.fold_in(jax.random.fold_in(own_key, 6), position), (blocks,), jnp.float32, least / len(cuts), high / len(cuts))
        gain = gain * jnp.repeat(jnp.exp(heights), dims[position] // blocks).reshape((-1,) + (1,) * (len(dims) - 1 - position))
    return gain


def scatter_about(rng, dims, spread, limit, cuts=(), dtype=jnp.bfloat16):
    array = spread * jax.random.normal(rng, dims, jnp.float32)
    if cuts:
        array = array * block_scale(rng, dims, cuts, -0.22, 0.18)
    return jnp.clip(array, -limit, limit).astype(dtype)


def setup_inputs(seed: int = 0) -> dict:
    seeds = jax.random.split(jax.random.key(seed), 9)
    sequence_stack = scatter_about(seeds[0], (ASSEMBLY_TOTAL, SEQUENCE_LIMIT, WINDOW_LENGTH, FEATURE_DEPTH), 1.0, 6.0, ((0, 8), (1, 32)))
    depths = draw_depths(jax.random.fold_in(seeds[8], 71), 0)
    standardize_factor = jnp.clip(1.0 + 0.18 * jax.random.normal(seeds[2], (FEATURE_DEPTH,), jnp.float32), 0.1, 1.9)
    standardize_shift = scatter_about(seeds[3], (FEATURE_DEPTH,), 0.3, 1.5, (), jnp.float32)
    input_weight = draw_input_weight(jax.random.fold_in(seeds[8], 71), 0)
    sigmoid_shift = scatter_about(seeds[5], (FEATURE_DEPTH,), 1.0, 4.0, (), jnp.float32)
    result_matrix = scatter_about(seeds[6], (FEATURE_DEPTH, FEATURE_DEPTH), FEATURE_DEPTH ** -0.5, 0.375, ((0, 8),))
    result_shift = scatter_about(seeds[7], (FEATURE_DEPTH,), 0.3, 1.5, (), jnp.float32)
    return dict(sequence_stack=sequence_stack, depths=depths, standardize_factor=standardize_factor, standardize_shift=standardize_shift, input_weight=input_weight, sigmoid_shift=sigmoid_shift, result_matrix=result_matrix, result_shift=result_shift)


def apply_layer_norm(values, standardize_factor, standardize_shift):
    values = values.astype(jnp.float32)
    average = lax.optimization_barrier(jnp.mean(values, -1, keepdims=True))
    variance = lax.optimization_barrier(jnp.mean(jnp.square(values - average), -1, keepdims=True))
    return ((values - average) * lax.rsqrt(variance + 1e-05) * standardize_factor + standardize_shift).astype(jnp.bfloat16)

def apply_projection(normed, input_weight, sigmoid_shift):
    channel_count = normed.shape[-1]
    product = jnp.dot(normed.reshape(-1, channel_count), input_weight, preferred_element_type=jnp.float32)
    gates = jax.nn.sigmoid(product[:, 3 * channel_count:] + sigmoid_shift)
    joined = jnp.concatenate([product[:, :3 * channel_count], gates], axis=1).astype(jnp.bfloat16)
    return joined.reshape(normed.shape[:-1] + (4 * channel_count,))

def column_attend(column, depth_now):
    channel_count = column.shape[-1] // 4
    path_dimension = channel_count // FOCUS_PATHS
    seq_rows = column.shape[0]
    widened = column.astype(jnp.float32)
    queries = widened[:, :channel_count].reshape(seq_rows, FOCUS_PATHS, path_dimension)
    key_rows = widened[:, channel_count:2 * channel_count].reshape(seq_rows, FOCUS_PATHS, path_dimension)
    value_rows = widened[:, 2 * channel_count:3 * channel_count].reshape(seq_rows, FOCUS_PATHS, path_dimension)
    gates = widened[:, 3 * channel_count:]
    scores = jnp.einsum('qhd,khd->hqk', queries, key_rows) * (1.0 / math.sqrt(path_dimension))
    live_keys = (jnp.arange(seq_rows) < depth_now)[None, None, :]
    scores = jnp.where(live_keys, scores, -1e+30)
    row_top = lax.optimization_barrier(jnp.max(scores, -1, keepdims=True))
    exponent = jnp.exp(scores - row_top)
    rounded = (exponent / lax.optimization_barrier(jnp.sum(exponent, -1, keepdims=True))).astype(jnp.bfloat16)
    rounded = lax.optimization_barrier(rounded)
    weights = rounded.astype(jnp.float32)
    mixture = jnp.einsum('hqk,khd->qhd', weights, value_rows).reshape(seq_rows, channel_count)
    return (gates * mixture).astype(jnp.bfloat16)

def reference(sequence_stack, depths, standardize_factor, standardize_shift, input_weight, sigmoid_shift, result_matrix, result_shift):

    def single_complex(packed):
        block_rows, depth_now = packed
        seq_rows, residue_count, channel_count = block_rows.shape
        joined = apply_projection(apply_layer_norm(block_rows, standardize_factor, standardize_shift), input_weight, sigmoid_shift)
        by_column = jnp.swapaxes(joined, 0, 1)

        def per_column(column):
            return column_attend(column, depth_now)
        gated_out = lax.map(per_column, by_column)
        gated_out = jnp.swapaxes(gated_out, 0, 1).reshape(-1, channel_count)
        row_update = jnp.dot(gated_out, result_matrix, preferred_element_type=jnp.float32).reshape(seq_rows, residue_count, channel_count) + result_shift
        keep_mask = (jnp.arange(seq_rows) < depth_now).astype(jnp.float32)[:, None, None]
        return (block_rows.astype(jnp.float32) + keep_mask * row_update).astype(jnp.bfloat16)
    return lax.map(single_complex, (sequence_stack, depths))
```

```python
from functools import partial
import math

import jax
import jax.numpy as jnp
from jax import lax
from jax.experimental import pallas as pl
from jax.experimental.pallas import tpu as pltpu
from jax.sharding import PartitionSpec as P

FOCUS_PATHS = 8
TILE = 16
SOFT_ROWS = 64
VMEM_LIMIT = 48 * 1024 * 1024
WIDTHS = ((4, 4), (4, 4))


def swap_matrix():
    to = lax.broadcasted_iota(jnp.int32, (TILE * TILE, TILE * TILE), 0)
    come = lax.broadcasted_iota(jnp.int32, (TILE * TILE, TILE * TILE), 1)
    return ((to % TILE) * TILE + to // TILE == come).astype(jnp.bfloat16)


def swap_tokens(permutation, tokens):
    return jnp.dot(permutation, tokens, preferred_element_type=jnp.float32).astype(jnp.bfloat16)


def pack_kernel(x_ref, o_ref):
    rows, homes, channels = x_ref.shape
    permutation = swap_matrix()
    for first in range(0, homes, TILE):
        tokens = x_ref[:, first : first + TILE, :].reshape(TILE * TILE, channels)
        swapped = swap_tokens(permutation, tokens)
        o_ref[first : first + TILE, 0] = swapped.reshape(TILE, rows, channels)


def unpack_kernel(y_ref, *rest):
    o_ref = rest[-1]
    rows, homes, channels = o_ref.shape
    permutation = swap_matrix()
    for first in range(0, homes, TILE):
        tokens = y_ref[first : first + TILE, 0].reshape(TILE * TILE, channels)
        swapped = swap_tokens(permutation, tokens)
        o_ref[:, first : first + TILE, :] = swapped.reshape(rows, TILE, channels)


def pack(rows, start, width, homes):
    complex_rows, _, channels = rows.shape
    return pl.pallas_call(
        pack_kernel,
        grid=(width,),
        in_specs=[pl.BlockSpec((complex_rows, homes, channels), lambda j: (0, start + j, 0))],
        out_specs=pl.BlockSpec((homes, 1, complex_rows, channels), lambda j: (0, j, 0, 0)),
        out_shape=jax.ShapeDtypeStruct((homes, width, complex_rows, channels), jnp.bfloat16),
        compiler_params=pltpu.CompilerParams(vmem_limit_bytes=VMEM_LIMIT),
        name="pack_columns",
    )(rows)


def unpack(returned, before, start, columns):
    homes, width, complex_rows, channels = returned.shape
    operands = [returned]
    in_specs = [pl.BlockSpec((homes, 1, complex_rows, channels), lambda j: (0, j, 0, 0))]
    aliases = {}
    if before is not None:
        operands.append(before)
        in_specs.append(pl.BlockSpec(memory_space=pl.ANY))
        aliases = {1: 0}
    return pl.pallas_call(
        unpack_kernel,
        grid=(width,),
        in_specs=in_specs,
        out_specs=pl.BlockSpec((complex_rows, homes, channels), lambda j: (0, start + j, 0)),
        out_shape=jax.ShapeDtypeStruct((complex_rows, columns, channels), jnp.bfloat16),
        input_output_aliases=aliases,
        compiler_params=pltpu.CompilerParams(vmem_limit_bytes=VMEM_LIMIT),
        name="unpack_columns",
    )(*operands)


def column_kernel(
    depth_ref, x_ref, parts_ref, result_ref, norm_ref, sigmoid_ref, shift_ref, o_ref,
    weight_ref, packed_ref, scores_ref, soft_ref
):
    ranks, _, rows, channels = x_ref.shape
    seq_rows = ranks * rows
    path_dimension = channels // FOCUS_PATHS
    depth = depth_ref[0]

    @pl.when(pl.program_id(0) == 0)
    def _():
        width = parts_ref.shape[2]
        for part in range(parts_ref.shape[0]):
            weight_ref[:, part * width : (part + 1) * width] = parts_ref[part]

    values = x_ref[:, 0].reshape(seq_rows, channels).astype(jnp.float32)
    average = jnp.mean(values, -1, keepdims=True)
    centred = values - average
    variance = jnp.mean(jnp.square(centred), -1, keepdims=True)
    normed = (
        centred * lax.rsqrt(variance + 1e-05) * norm_ref[0:1] + norm_ref[1:2]
    ).astype(jnp.bfloat16)
    product = jnp.dot(normed, weight_ref[...], preferred_element_type=jnp.float32)
    packed_ref[:, : 3 * channels] = product[:, : 3 * channels].astype(jnp.bfloat16)
    gates = jax.nn.sigmoid(product[:, 3 * channels :] + sigmoid_ref[...])
    packed_ref[:, 3 * channels :] = gates.astype(jnp.bfloat16)

    keys_t = packed_ref[:, channels : 2 * channels].T
    dead = lax.broadcasted_iota(jnp.int32, (1, seq_rows), 1) >= depth
    head_of = lax.broadcasted_iota(jnp.int32, (1, channels), 1) // path_dimension
    scaling = math.log2(math.e) / math.sqrt(path_dimension)

    def score(head):
        queries = packed_ref[:, :channels]
        own = jnp.where(head_of == head, queries, jnp.zeros_like(queries))
        scores_ref[head % 2] = jnp.dot(own, keys_t, preferred_element_type=jnp.float32)

    def soften(head):
        for first in range(0, seq_rows, SOFT_ROWS):
            scores = jnp.where(dead, -1e30, scores_ref[head % 2, first : first + SOFT_ROWS])
            row_top = jnp.max(scores, -1, keepdims=True) * scaling
            exponent = jnp.exp2(scores * scaling - row_top)
            total = jnp.sum(exponent, -1, keepdims=True)
            soft_ref[head % 2, first : first + SOFT_ROWS] = (exponent * (1.0 / total)).astype(
                jnp.bfloat16
            )

    half = channels // 2
    mixtures = [jnp.zeros((seq_rows, half), jnp.float32)] * 2

    def mix(head):
        side = head * path_dimension // half
        value_rows = packed_ref[:, 2 * channels + side * half : 2 * channels + (side + 1) * half]
        mixed = jnp.dot(soft_ref[head % 2], value_rows, preferred_element_type=jnp.float32)
        own = head_of[:, side * half : (side + 1) * half] == head
        mixtures[side] = jnp.where(own, mixed, mixtures[side])

    score(0)
    for head in range(FOCUS_PATHS):
        if head + 1 < FOCUS_PATHS:
            score(head + 1)
        soften(head)
        if head > 0:
            mix(head - 1)
    mix(FOCUS_PATHS - 1)

    gate_rows = packed_ref[:, 3 * channels :].astype(jnp.float32)
    gated = (gate_rows * jnp.concatenate(mixtures, 1)).astype(jnp.bfloat16)
    update = jnp.dot(gated, result_ref[...], preferred_element_type=jnp.float32) + shift_ref[...]
    live = lax.broadcasted_iota(jnp.int32, (seq_rows, 1), 0) < depth
    update = jnp.where(live, 1.0, 0.0) * update
    changed = x_ref[:, 0].reshape(seq_rows, channels).astype(jnp.float32) + update
    o_ref[:, 0] = changed.astype(jnp.bfloat16).reshape(ranks, rows, channels)


def attend(arrived, own_depth, parts, result, norm, sigmoid, shift):
    ranks, per, rows, channels = arrived.shape
    seq_rows = ranks * rows
    whole = lambda a: pl.BlockSpec(a.shape, lambda i, *_: (0,) * a.ndim)
    column = pl.BlockSpec((ranks, 1, rows, channels), lambda i, *_: (0, i, 0, 0))
    return pl.pallas_call(
        column_kernel,
        grid_spec=pltpu.PrefetchScalarGridSpec(
            num_scalar_prefetch=1,
            grid=(per,),
            in_specs=[column] + [whole(a) for a in (parts, result, norm, sigmoid, shift)],
            out_specs=column,
            scratch_shapes=[
                pltpu.VMEM((channels, 4 * channels), jnp.bfloat16),
                pltpu.VMEM((seq_rows, 4 * channels), jnp.bfloat16),
                pltpu.VMEM((2, seq_rows, seq_rows), jnp.float32),
                pltpu.VMEM((2, seq_rows, seq_rows), jnp.bfloat16),
            ],
        ),
        out_shape=jax.ShapeDtypeStruct(arrived.shape, jnp.bfloat16),
        compiler_params=pltpu.CompilerParams(vmem_limit_bytes=VMEM_LIMIT),
        cost_estimate=pl.CostEstimate(
            flops=per * seq_rows * channels * (10 * channels + 4 * FOCUS_PATHS * seq_rows),
            bytes_accessed=4 * per * seq_rows * channels,
            transcendentals=per * FOCUS_PATHS * seq_rows * seq_rows,
        ),
        name="attend_columns",
    )(own_depth, arrived, parts, result, norm, sigmoid, shift)


def exchange(blocks):
    return lax.all_to_all(blocks, "grp", split_axis=0, concat_axis=0, tiled=True)


def chunked(rows, own_depth, gathered, vectors, homes, widths):
    _, columns, channels = rows.shape
    later, gathered = lax.optimization_barrier((rows, gathered))
    parts = gathered[:, :channels]
    result = gathered[:, channels:].reshape(channels, channels)
    starts = [sum(widths[:i]) for i in range(len(widths))]
    arrived = [
        exchange(pack(later if s else rows, s, w, homes)) for s, w in zip(starts, widths)
    ]
    out = None
    for start, blocks in zip(starts, arrived):
        done = exchange(attend(blocks, own_depth, parts, result, *vectors))
        out = unpack(done, out, start, columns)
    return out


def shards(
    sequence_stack,
    depths,
    standardize_factor,
    standardize_shift,
    input_weight,
    sigmoid_shift,
    result_matrix,
    result_shift,
):
    rows = sequence_stack[0]
    complex_rows, columns, channels = rows.shape
    homes = lax.axis_size("grp")
    team = lax.axis_index("cplx")
    teams = lax.axis_size("cplx")
    own_depth = lax.dynamic_slice(depths, (team,), (1,))
    norm = jnp.stack([standardize_factor, standardize_shift])
    vectors = (norm, sigmoid_shift[None], result_shift[None])
    width = input_weight.shape[1]
    both = jnp.concatenate([input_weight, result_matrix.reshape(-1, width)], axis=0)
    other = lax.ppermute(both, "cplx", [(c, c ^ 1) for c in range(teams)])
    own_core = [list(range(core, teams, 2)) for core in range(2)]

    def run(core, rows, both, other):
        pair = jnp.stack([both, other] if core == 0 else [other, both])
        gathered = lax.all_gather(pair, "cplx", axis=0, tiled=True, axis_index_groups=own_core)
        if core == 1:
            rows, gathered = lax.optimization_barrier((rows, gathered))
        return chunked(rows, own_depth, gathered, vectors, homes, WIDTHS[core])

    return lax.cond(team % 2 == 0, partial(run, 0), partial(run, 1), rows, both, other)[None]


def solution(mesh):
    placed = (
        P("cplx", "grp", None, None),
        P(),
        P(),
        P(),
        P(None, "cplx"),
        P(),
        P("cplx", None),
        P(),
    )
    return jax.shard_map(
        shards, mesh=mesh, in_specs=placed, out_specs=P("cplx", "grp", None, None), check_vma=False
    )
```

```python
from functools import partial
import math

import jax
import jax.numpy as jnp
from jax import lax
from jax.experimental import pallas as pl
from jax.experimental.pallas import tpu as pltpu
from jax.sharding import PartitionSpec as P

FOCUS_PATHS = 8
PAIRS = ((0, 2), (1, 3), (4, 6), (5, 7))
TILE = 16
SOFT_ROWS = 64
VMEM_LIMIT = 48 * 1024 * 1024
SENT = ((8,), (4, 4))
BACK = ((4, 4), (4, 4))


def swap_matrix():
    to = lax.broadcasted_iota(jnp.int32, (TILE * TILE, 1), 0)
    come = lax.broadcasted_iota(jnp.int32, (1, TILE * TILE), 1)
    return ((to & (TILE - 1)) * TILE + (to >> 4) == come).astype(jnp.bfloat16)


def swap_tokens(permutation, tokens):
    return jnp.dot(permutation, tokens, preferred_element_type=jnp.float32).astype(jnp.bfloat16)


def pack_kernel(x_ref, o_ref):
    rows, columns, channels = x_ref.shape
    homes = o_ref.shape[0]
    permutation = swap_matrix()
    for first in range(0, columns, TILE):
        tokens = x_ref[:, first : first + TILE, :].reshape(TILE * TILE, channels)
        swapped = swap_tokens(permutation, tokens)
        home = first % homes
        o_ref[home : home + TILE, first // homes] = swapped.reshape(TILE, rows, channels)


def unpack_kernel(y_ref, *rest):
    o_ref = rest[-1]
    rows, columns, channels = o_ref.shape
    homes = y_ref.shape[0]
    permutation = swap_matrix()
    for first in range(0, columns, TILE):
        home = first % homes
        tokens = y_ref[home : home + TILE, first // homes].reshape(TILE * TILE, channels)
        swapped = swap_tokens(permutation, tokens)
        o_ref[:, first : first + TILE, :] = swapped.reshape(rows, TILE, channels)


def step_of(start, width):
    return 2 if start % 2 == 0 and width % 2 == 0 else 1


def pack(rows, start, width, homes):
    complex_rows, _, channels = rows.shape
    step = step_of(start, width)
    return pl.pallas_call(
        pack_kernel,
        grid=(width // step,),
        in_specs=[
            pl.BlockSpec((complex_rows, step * homes, channels), lambda j: (0, start // step + j, 0))
        ],
        out_specs=pl.BlockSpec((homes, step, complex_rows, channels), lambda j: (0, j, 0, 0)),
        out_shape=jax.ShapeDtypeStruct((homes, width, complex_rows, channels), jnp.bfloat16),
        compiler_params=pltpu.CompilerParams(vmem_limit_bytes=VMEM_LIMIT),
        name="pack_columns",
    )(rows)


def unpack(returned, before, start, columns):
    homes, width, complex_rows, channels = returned.shape
    step = step_of(start, width)
    operands = [returned]
    in_specs = [pl.BlockSpec((homes, step, complex_rows, channels), lambda j: (0, j, 0, 0))]
    aliases = {}
    if before is not None:
        operands.append(before)
        in_specs.append(pl.BlockSpec(memory_space=pl.ANY))
        aliases = {1: 0}
    return pl.pallas_call(
        unpack_kernel,
        grid=(width // step,),
        in_specs=in_specs,
        out_specs=pl.BlockSpec(
            (complex_rows, step * homes, channels), lambda j: (0, start // step + j, 0)
        ),
        out_shape=jax.ShapeDtypeStruct((complex_rows, columns, channels), jnp.bfloat16),
        input_output_aliases=aliases,
        compiler_params=pltpu.CompilerParams(vmem_limit_bytes=VMEM_LIMIT),
        name="unpack_columns",
    )(*operands)


def column_kernel(
    depths_ref, team_ref, x_ref, parts_ref, result_ref, factor_ref, offset_ref, sigmoid_ref, shift_ref, o_ref,
    weight_ref, packed_ref, keys_ref, own_ref, scores_ref, soft_ref
):
    ranks, _, rows, channels = x_ref.shape
    seq_rows = ranks * rows
    path_dimension = channels // FOCUS_PATHS
    depth = depths_ref[team_ref[0]]

    @pl.when(pl.program_id(0) == 0)
    def _():
        width = parts_ref.shape[2]
        for part in range(parts_ref.shape[0]):
            weight_ref[:, part * width : (part + 1) * width] = parts_ref[part]

    values = x_ref[:, 0].reshape(seq_rows, channels).astype(jnp.float32)
    average = jnp.mean(values, -1, keepdims=True)
    centred = values - average
    variance = jnp.mean(jnp.square(centred), -1, keepdims=True)
    normed = (
        centred * lax.rsqrt(variance + 1e-05) * factor_ref[...] + offset_ref[...]
    ).astype(jnp.bfloat16)
    product = jnp.dot(normed, weight_ref[...], preferred_element_type=jnp.float32)
    packed_ref[:, : 3 * channels] = product[:, : 3 * channels].astype(jnp.bfloat16)
    gates = jax.nn.sigmoid(product[:, 3 * channels :] + sigmoid_ref[...])
    packed_ref[:, 3 * channels :] = gates.astype(jnp.bfloat16)

    keys_t = packed_ref[:, channels : 2 * channels].T
    lane = lax.broadcasted_iota(jnp.int32, (1, channels), 1)
    channel = lax.broadcasted_iota(jnp.int32, (channels, 1), 0)
    dead = lax.broadcasted_iota(jnp.int32, (1, seq_rows), 1) >= depth
    mask = jnp.where(dead, -1e30, 0.0).astype(jnp.bfloat16)
    for odd in range(2):
        spare = channel % (2 * path_dimension) == (1 - odd) * path_dimension
        keys_ref[odd] = jnp.where(spare, mask, keys_t)
    scaling = math.log2(math.e) / math.sqrt(path_dimension)
    half = channels // 2
    mixtures = [jnp.zeros((seq_rows, half), jnp.float32)] * 2

    def score(index):
        queries = packed_ref[:, :channels]
        for place, head in enumerate(PAIRS[index]):
            other = jnp.where(lane == (head ^ 1) * path_dimension, 1.0, 0.0).astype(jnp.bfloat16)
            own_ref[index % 2, place * seq_rows : (place + 1) * seq_rows] = jnp.where(
                lane // path_dimension == head, queries, other
            )
        scores_ref[index % 2] = jnp.dot(
            own_ref[index % 2], keys_ref[PAIRS[index][0] % 2], preferred_element_type=jnp.float32
        )

    def soften(index):
        for first in range(0, len(PAIRS[index]) * seq_rows, SOFT_ROWS):
            scores = scores_ref[index % 2, first : first + SOFT_ROWS]
            row_top = jnp.max(scores, -1, keepdims=True) * scaling
            exponent = jnp.exp2(scores * scaling - row_top)
            total = jnp.sum(exponent, -1, keepdims=True)
            soft_ref[index % 2, first : first + SOFT_ROWS] = (exponent * (1.0 / total)).astype(
                jnp.bfloat16
            )

    def mix(index):
        side = PAIRS[index][0] * path_dimension // half
        value_rows = packed_ref[:, 2 * channels + side * half : 2 * channels + (side + 1) * half]
        mixed = jnp.dot(soft_ref[index % 2], value_rows, preferred_element_type=jnp.float32)
        for place, head in enumerate(PAIRS[index]):
            own = lane[:, side * half : (side + 1) * half] // path_dimension == head
            mixtures[side] = jnp.where(
                own, mixed[place * seq_rows : (place + 1) * seq_rows], mixtures[side]
            )

    score(0)
    for index in range(len(PAIRS)):
        if index + 1 < len(PAIRS):
            score(index + 1)
        soften(index)
        if index > 0:
            mix(index - 1)
    mix(len(PAIRS) - 1)

    gate_rows = packed_ref[:, 3 * channels :].astype(jnp.float32)
    gated = (gate_rows * jnp.concatenate(mixtures, 1)).astype(jnp.bfloat16)
    update = jnp.dot(gated, result_ref[...], preferred_element_type=jnp.float32) + shift_ref[...]
    live = lax.broadcasted_iota(jnp.int32, (seq_rows, 1), 0) < depth
    update = jnp.where(live, 1.0, 0.0) * update
    changed = x_ref[:, 0].reshape(seq_rows, channels).astype(jnp.float32) + update
    o_ref[:, 0] = changed.astype(jnp.bfloat16).reshape(ranks, rows, channels)


def attend(arrived, start, width, scalars, params):
    ranks, _, rows, channels = arrived.shape
    seq_rows = ranks * rows

    def whole(a):
        return pl.BlockSpec(a.shape, lambda *_: (0,) * len(a.shape))

    return pl.pallas_call(
        column_kernel,
        grid_spec=pltpu.PrefetchScalarGridSpec(
            num_scalar_prefetch=len(scalars),
            grid=(width,),
            in_specs=[pl.BlockSpec((ranks, 1, rows, channels), lambda i, *_: (0, start + i, 0, 0))]
            + [whole(a) for a in params],
            out_specs=pl.BlockSpec((ranks, 1, rows, channels), lambda i, *_: (0, i, 0, 0)),
            scratch_shapes=[
                pltpu.VMEM((channels, 4 * channels), jnp.bfloat16),
                pltpu.VMEM((seq_rows, 4 * channels), jnp.bfloat16),
                pltpu.VMEM((2, channels, seq_rows), jnp.bfloat16),
                pltpu.VMEM((2, 2 * seq_rows, channels), jnp.bfloat16),
                pltpu.VMEM((2, 2 * seq_rows, seq_rows), jnp.float32),
                pltpu.VMEM((2, 2 * seq_rows, seq_rows), jnp.bfloat16),
            ],
        ),
        out_shape=jax.ShapeDtypeStruct((ranks, width, rows, channels), jnp.bfloat16),
        compiler_params=pltpu.CompilerParams(vmem_limit_bytes=VMEM_LIMIT),
        cost_estimate=pl.CostEstimate(
            flops=width * seq_rows * channels * (10 * channels + 4 * FOCUS_PATHS * seq_rows),
            bytes_accessed=4 * width * seq_rows * channels,
            transcendentals=width * FOCUS_PATHS * seq_rows * seq_rows,
        ),
        name="attend_columns",
    )(*scalars, arrived, *params)


def exchange(blocks):
    return lax.all_to_all(blocks, "grp", split_axis=0, concat_axis=0, tiled=True)


def chunked(rows, scalars, gathered, vectors, homes, sent, back):
    _, columns, channels = rows.shape
    later, gathered = lax.optimization_barrier((rows, gathered))
    params = (gathered[:, :channels], gathered[:, channels:].reshape(channels, channels), *vectors)
    arrived, first = [], 0
    for width in sent:
        arrived.append((first, exchange(pack(later if first else rows, first, width, homes))))
        first += width
    out, first = None, 0
    for width in back:
        begin, blocks = [a for a in arrived if a[0] <= first][-1]
        done = exchange(attend(blocks, first - begin, width, scalars, params))
        out = unpack(done, out, first, columns)
        first += width
    return out


def shards(
    sequence_stack,
    depths,
    standardize_factor,
    standardize_shift,
    input_weight,
    sigmoid_shift,
    result_matrix,
    result_shift,
):
    homes = lax.axis_size("grp")
    team = lax.axis_index("cplx")
    teams = lax.axis_size("cplx")
    vectors = [standardize_factor, standardize_shift, sigmoid_shift, result_shift]
    vectors = [vector.reshape(1, -1) for vector in vectors]
    scalars = (depths, team.astype(jnp.int32).reshape(1))
    own = (input_weight, result_matrix)
    other = lax.ppermute(own, "cplx", [(c, c ^ 1) for c in range(teams)])
    own_core = [list(range(core, teams, 2)) for core in range(2)]

    def run(core, rows, own, other):
        def flat(shard):
            return jnp.concatenate([shard[0], shard[1].reshape(-1, shard[0].shape[1])], axis=0)

        pair = jnp.stack([flat(own), flat(other)] if core == 0 else [flat(other), flat(own)])
        gathered = lax.all_gather(pair, "cplx", axis=0, tiled=True, axis_index_groups=own_core)
        return chunked(rows, scalars, gathered, vectors, homes, SENT[core], BACK[core])

    runs = [partial(run, core) for core in range(2)]
    return lax.cond(team % 2 == 0, *runs, sequence_stack[0], own, other)[None]


def solution(mesh):
    placed = (
        P("cplx", "grp", None, None),
        P(),
        P(),
        P(),
        P(None, "cplx"),
        P(),
        P("cplx", None),
        P(),
    )
    return jax.shard_map(
        shards, mesh=mesh, in_specs=placed, out_specs=P("cplx", "grp", None, None), check_vma=False
    )
```

```python
from functools import partial
import math

import jax
import jax.numpy as jnp
from jax import lax
from jax.experimental import pallas as pl
from jax.experimental.pallas import tpu as pltpu
from jax.sharding import PartitionSpec as P

FOCUS_PATHS = 8
PAIRS = ((0, 2), (1, 3), (4, 6), (5, 7))
TILE = 16
SOFT_ROWS = 64
VMEM_LIMIT = 32 * 1024 * 1024
AT_ONCE = (1, 1)
SENT = ((8,), (4, 4))
BACK = ((4, 4), (4, 4))


def swap_matrix():
    to = lax.broadcasted_iota(jnp.int32, (TILE * TILE, 1), 0)
    come = lax.broadcasted_iota(jnp.int32, (1, TILE * TILE), 1)
    return ((to & (TILE - 1)) * TILE + (to >> 4) == come).astype(jnp.bfloat16)


def swap_tokens(permutation, tokens):
    return jnp.dot(permutation, tokens, preferred_element_type=jnp.float32).astype(jnp.bfloat16)


def pack_kernel(x_ref, o_ref):
    rows, columns, channels = x_ref.shape
    homes = o_ref.shape[0]
    permutation = swap_matrix()
    for first in range(0, columns, TILE):
        tokens = x_ref[:, first : first + TILE, :].reshape(TILE * TILE, channels)
        swapped = swap_tokens(permutation, tokens)
        home = first % homes
        o_ref[home : home + TILE, first // homes] = swapped.reshape(TILE, rows, channels)


def unpack_kernel(y_ref, *rest):
    o_ref = rest[-1]
    rows, columns, channels = o_ref.shape
    homes = y_ref.shape[0]
    permutation = swap_matrix()
    for first in range(0, columns, TILE):
        home = first % homes
        tokens = y_ref[home : home + TILE, first // homes].reshape(TILE * TILE, channels)
        swapped = swap_tokens(permutation, tokens)
        o_ref[:, first : first + TILE, :] = swapped.reshape(rows, TILE, channels)


def step_of(start, width):
    return 2 if start % 2 == 0 and width % 2 == 0 else 1


def pack(rows, start, width, homes):
    complex_rows, _, channels = rows.shape
    step = step_of(start, width)
    return pl.pallas_call(
        pack_kernel,
        grid=(width // step,),
        in_specs=[
            pl.BlockSpec((complex_rows, step * homes, channels), lambda j: (0, start // step + j, 0))
        ],
        out_specs=pl.BlockSpec((homes, step, complex_rows, channels), lambda j: (0, j, 0, 0)),
        out_shape=jax.ShapeDtypeStruct((homes, width, complex_rows, channels), jnp.bfloat16),
        compiler_params=pltpu.CompilerParams(vmem_limit_bytes=VMEM_LIMIT),
        name="pack_columns",
    )(rows)


def unpack(returned, before, start, columns):
    homes, width, complex_rows, channels = returned.shape
    step = step_of(start, width)
    operands = [returned]
    in_specs = [pl.BlockSpec((homes, step, complex_rows, channels), lambda j: (0, j, 0, 0))]
    aliases = {}
    if before is not None:
        operands.append(before)
        in_specs.append(pl.BlockSpec(memory_space=pl.ANY))
        aliases = {1: 0}
    return pl.pallas_call(
        unpack_kernel,
        grid=(width // step,),
        in_specs=in_specs,
        out_specs=pl.BlockSpec(
            (complex_rows, step * homes, channels), lambda j: (0, start // step + j, 0)
        ),
        out_shape=jax.ShapeDtypeStruct((complex_rows, columns, channels), jnp.bfloat16),
        input_output_aliases=aliases,
        compiler_params=pltpu.CompilerParams(vmem_limit_bytes=VMEM_LIMIT),
        name="unpack_columns",
    )(*operands)


def column_kernel(
    columns, depths_ref, team_ref, x_ref, parts_ref, result_ref, factor_ref, offset_ref, sigmoid_ref, shift_ref, o_ref,
    weight_ref, packed_ref, keys_ref, own_ref, scores_ref, soft_ref
):
    ranks, _, rows, channels = x_ref.shape
    seq_rows = ranks * rows
    path_dimension = channels // FOCUS_PATHS
    depth = depths_ref[team_ref[0]]

    @pl.when(pl.program_id(0) == 0)
    def _():
        width = parts_ref.shape[2]
        for part in range(parts_ref.shape[0]):
            weight_ref[:, part * width : (part + 1) * width] = parts_ref[part]

    lane = lax.broadcasted_iota(jnp.int32, (1, channels), 1)
    channel = lax.broadcasted_iota(jnp.int32, (channels, 1), 0)
    dead = lax.broadcasted_iota(jnp.int32, (1, seq_rows), 1) >= depth
    mask = jnp.where(dead, -1e30, 0.0).astype(jnp.bfloat16)
    scaling = math.log2(math.e) / math.sqrt(path_dimension)
    half = channels // 2
    count = len(PAIRS)
    mixtures = [[jnp.zeros((seq_rows, half), jnp.float32)] * 2 for _ in range(columns)]

    def project(column):
        values = x_ref[:, column].reshape(seq_rows, channels).astype(jnp.float32)
        average = jnp.mean(values, -1, keepdims=True)
        centred = values - average
        variance = jnp.mean(jnp.square(centred), -1, keepdims=True)
        normed = (
            centred * lax.rsqrt(variance + 1e-05) * factor_ref[...] + offset_ref[...]
        ).astype(jnp.bfloat16)
        product = jnp.dot(normed, weight_ref[...], preferred_element_type=jnp.float32)
        packed_ref[column, :, : 3 * channels] = product[:, : 3 * channels].astype(jnp.bfloat16)
        gates = jax.nn.sigmoid(product[:, 3 * channels :] + sigmoid_ref[...])
        packed_ref[column, :, 3 * channels :] = gates.astype(jnp.bfloat16)

        keys_t = packed_ref[column, :, channels : 2 * channels].T
        for odd in range(2):
            spare = channel % (2 * path_dimension) == (1 - odd) * path_dimension
            keys_ref[column, odd] = jnp.where(spare, mask, keys_t)

    def score(index):
        column, pair = index // count, PAIRS[index % count]
        queries = packed_ref[column, :, :channels]
        for place, head in enumerate(pair):
            other = jnp.where(lane == (head ^ 1) * path_dimension, 1.0, 0.0).astype(jnp.bfloat16)
            own_ref[index % 2, place * seq_rows : (place + 1) * seq_rows] = jnp.where(
                lane // path_dimension == head, queries, other
            )
        scores_ref[index % 2] = jnp.dot(
            own_ref[index % 2], keys_ref[column, pair[0] % 2], preferred_element_type=jnp.float32
        )

    def soften(index):
        for first in range(0, len(PAIRS[0]) * seq_rows, SOFT_ROWS):
            scores = scores_ref[index % 2, first : first + SOFT_ROWS]
            row_top = jnp.max(scores, -1, keepdims=True) * scaling
            exponent = jnp.exp2(scores * scaling - row_top)
            total = jnp.sum(exponent, -1, keepdims=True)
            soft_ref[index % 2, first : first + SOFT_ROWS] = (exponent * (1.0 / total)).astype(
                jnp.bfloat16
            )

    def mix(index):
        column, pair = index // count, PAIRS[index % count]
        side = pair[0] * path_dimension // half
        value_rows = packed_ref[column, :, 2 * channels + side * half : 2 * channels + (side + 1) * half]
        mixed = jnp.dot(soft_ref[index % 2], value_rows, preferred_element_type=jnp.float32)
        for place, head in enumerate(pair):
            own = lane[:, side * half : (side + 1) * half] // path_dimension == head
            mixtures[column][side] = jnp.where(
                own, mixed[place * seq_rows : (place + 1) * seq_rows], mixtures[column][side]
            )

    def finish(column):
        gate_rows = packed_ref[column, :, 3 * channels :].astype(jnp.float32)
        gated = (gate_rows * jnp.concatenate(mixtures[column], 1)).astype(jnp.bfloat16)
        update = jnp.dot(gated, result_ref[...], preferred_element_type=jnp.float32) + shift_ref[...]
        live = lax.broadcasted_iota(jnp.int32, (seq_rows, 1), 0) < depth
        update = jnp.where(live, 1.0, 0.0) * update
        changed = x_ref[:, column].reshape(seq_rows, channels).astype(jnp.float32) + update
        o_ref[:, column] = changed.astype(jnp.bfloat16).reshape(ranks, rows, channels)

    project(0)
    score(0)
    total_count = columns * count
    for index in range(total_count):
        following = index + 1
        if following < total_count:
            score(following)
            if index % count == 1 and index // count + 1 < columns:
                project(index // count + 1)
        soften(index)
        if index > 0:
            mix(index - 1)
            if index % count == 0:
                finish(index // count - 1)
    mix(total_count - 1)
    finish(columns - 1)


def attend(arrived, start, width, columns, scalars, params):
    ranks, _, rows, channels = arrived.shape
    seq_rows = ranks * rows

    def whole(a):
        return pl.BlockSpec(a.shape, lambda *_: (0,) * len(a.shape))

    return pl.pallas_call(
        partial(column_kernel, columns),
        grid_spec=pltpu.PrefetchScalarGridSpec(
            num_scalar_prefetch=len(scalars),
            grid=(width // columns,),
            in_specs=[
                pl.BlockSpec((ranks, columns, rows, channels), lambda i, *_: (0, start // columns + i, 0, 0))
            ]
            + [whole(a) for a in params],
            out_specs=pl.BlockSpec((ranks, columns, rows, channels), lambda i, *_: (0, i, 0, 0)),
            scratch_shapes=[
                pltpu.VMEM((channels, 4 * channels), jnp.bfloat16),
                pltpu.VMEM((columns, seq_rows, 4 * channels), jnp.bfloat16),
                pltpu.VMEM((columns, 2, channels, seq_rows), jnp.bfloat16),
                pltpu.VMEM((2, 2 * seq_rows, channels), jnp.bfloat16),
                pltpu.VMEM((2, 2 * seq_rows, seq_rows), jnp.float32),
                pltpu.VMEM((2, 2 * seq_rows, seq_rows), jnp.bfloat16),
            ],
        ),
        out_shape=jax.ShapeDtypeStruct((ranks, width, rows, channels), jnp.bfloat16),
        compiler_params=pltpu.CompilerParams(vmem_limit_bytes=VMEM_LIMIT),
        cost_estimate=pl.CostEstimate(
            flops=width * seq_rows * channels * (10 * channels + 4 * FOCUS_PATHS * seq_rows),
            bytes_accessed=4 * width * seq_rows * channels,
            transcendentals=width * FOCUS_PATHS * seq_rows * seq_rows,
        ),
        name="attend_columns",
    )(*scalars, arrived, *params)


def exchange(blocks):
    return lax.all_to_all(blocks, "grp", split_axis=0, concat_axis=0, tiled=True)


def chunked(rows, scalars, gathered, vectors, homes, core):
    _, columns, channels = rows.shape
    later, gathered = lax.optimization_barrier((rows, gathered))
    params = (gathered[:, :channels], gathered[:, channels:].reshape(channels, channels), *vectors)
    arrived, first = [], 0
    for width in SENT[core]:
        arrived.append((first, exchange(pack(later if first else rows, first, width, homes))))
        first += width
    out, first = None, 0
    for width in BACK[core]:
        begin, blocks = [a for a in arrived if a[0] <= first][-1]
        done = exchange(attend(blocks, first - begin, width, AT_ONCE[core], scalars, params))
        out = unpack(done, out, first, columns)
        first += width
    return out


def shards(
    sequence_stack,
    depths,
    standardize_factor,
    standardize_shift,
    input_weight,
    sigmoid_shift,
    result_matrix,
    result_shift,
):
    homes = lax.axis_size("grp")
    team = lax.axis_index("cplx")
    teams = lax.axis_size("cplx")
    vectors = [standardize_factor, standardize_shift, sigmoid_shift, result_shift]
    vectors = [vector.reshape(1, -1) for vector in vectors]
    scalars = (depths, team.astype(jnp.int32).reshape(1))
    own = (input_weight, result_matrix)
    other = lax.ppermute(own, "cplx", [(c, c ^ 1) for c in range(teams)])
    own_core = [list(range(core, teams, 2)) for core in range(2)]

    def run(core, rows, own, other):
        def flat(shard):
            return jnp.concatenate([shard[0], shard[1].reshape(-1, shard[0].shape[1])], axis=0)

        pair = jnp.stack([flat(own), flat(other)] if core == 0 else [flat(other), flat(own)])
        gathered = lax.all_gather(pair, "cplx", axis=0, tiled=True, axis_index_groups=own_core)
        return chunked(rows, scalars, gathered, vectors, homes, core)

    runs = [partial(run, core) for core in range(2)]
    return lax.cond(team % 2 == 0, *runs, sequence_stack[0], own, other)[None]


def solution(mesh):
    placed = (
        P("cplx", "grp", None, None),
        P(),
        P(),
        P(),
        P(None, "cplx"),
        P(),
        P("cplx", None),
        P(),
    )
    return jax.shard_map(
        shards, mesh=mesh, in_specs=placed, out_specs=P("cplx", "grp", None, None), check_vma=False
    )
```
